128 devices in a mesh: row: 16 (over x, y), col: 8 (over z, core).
Axes of the slice: x: 4, y: 4, z: 4, core: 2. Of those that a mesh axis runs over, the one named last changes fastest.
Arguments:
- inputs: bfloat16 [512, 10240], P('col', 'row'), may hold values from -6 to 6
- cotangent: bfloat16 [512, 10240], P('col', 'row'), may hold values from -1.5 to 1.5
- w_in: bfloat16 [10240, 40960], P('row', 'col'), may hold values from -0.0625 to 0.0625
- w_out: bfloat16 [40960, 10240], P('col', 'row'), may hold values from -0.03125 to 0.03125
Outputs:
- grad_inputs: bfloat16 [512, 10240], P('col', 'row')
- grad_w_in: bfloat16 [10240, 40960], P('row', 'col')
- grad_w_out: bfloat16 [40960, 10240], P('col', 'row')
The draws below stay inside these ranges and needn't reach their ends.
All inputs are finite; a program needn't handle non-finite values.
Results may differ from the reference program's by a relative error of at most 0.028.
Values may be sent and summed in bfloat16 or wider, within the bound.
No kernel may reach another device: no remote copies, remote signals or barrier semaphores. Data moves between devices by JAX's collectives and lax.ppermute only.
A program may use at most 128 MiB of HBM per device.

```python
import math
import jax
import jax.numpy as jnp
from jax import lax

D = 10240
FF = 40960
TOKENS = 512
N_ROW = 16


def levels(stream_key, dims, cuts, low, top_value):
    loudness = 1.0
    for position, shards_of in cuts:
        steps = jax.random.uniform(jax.random.fold_in(jax.random.fold_in(stream_key, 6), position), (shards_of,), jnp.float32, low / len(cuts), top_value / len(cuts))
        loudness = loudness * jnp.repeat(jnp.exp(steps), dims[position] // shards_of).reshape((-1,) + (1,) * (len(dims) - 1 - position))
    return loudness


def gaussian(rng, extent, spread, limit, pieces=(), dtype=jnp.bfloat16):
    level = levels(rng, extent, pieces, -0.22, 0.18) if pieces else 1.0
    result = jax.random.normal(rng, extent, jnp.float32) * spread * level
    return jnp.minimum(jnp.maximum(result, -limit), limit).astype(dtype)


def setup_inputs(seed: int = 0) -> dict:
    splits = jax.random.split(jax.random.key(seed), 5)
    return {
        "inputs": gaussian(splits[0], (TOKENS, D), 1.0, 6.0, ((0, 8), (1, 16))),
        "cotangent": gaussian(splits[1], (TOKENS, D), 0.25, 1.5, ((0, 8), (1, 16))),
        "w_in": gaussian(splits[2], (D, FF), D ** -0.5, 0.0625, ((0, 16), (1, 8))),
        "w_out": gaussian(splits[3], (FF, D), FF ** -0.5, 0.03125, ((0, 8), (1, 16))),
    }


def gelu_parts(hidden):
    normal_cdf = 0.5 * (1.0 + jax.scipy.special.erf(hidden / math.sqrt(2.0)))
    density = jnp.exp(-0.5 * hidden * hidden) / math.sqrt(2.0 * math.pi)
    return (hidden * normal_cdf, normal_cdf + hidden * density)

def blocked_sum(left, right, right_dim):
    block_width = left.shape[1] // N_ROW
    other = right.shape[1 - right_dim]

    def add_block(index, total):
        left_block = lax.dynamic_slice_in_dim(left, index * block_width, block_width, 1)
        right_block = lax.dynamic_slice_in_dim(right, index * block_width, block_width, right_dim)
        term = lax.dot_general(left_block, right_block, (((1,), (right_dim,)), ((), ())), preferred_element_type=jnp.float32)
        rounded = lax.optimization_barrier(term.astype(jnp.bfloat16))
        return total + rounded.astype(jnp.float32)
    start_total = jnp.zeros((left.shape[0], other), jnp.float32)
    return lax.fori_loop(0, N_ROW, add_block, start_total)

def reference(inputs, cotangent, w_in, w_out):
    hidden = blocked_sum(inputs, w_in, 0)
    grad_act = blocked_sum(cotangent, w_out, 1)
    activated, derivative = gelu_parts(hidden)
    activated = activated.astype(jnp.bfloat16)
    grad_hidden = (grad_act * derivative).astype(jnp.bfloat16)
    grad_w_out = lax.dot_general(activated, cotangent, (((0,), (0,)), ((), ())), preferred_element_type=jnp.float32).astype(jnp.bfloat16)
    grad_w_in = lax.dot_general(inputs, grad_hidden, (((0,), (0,)), ((), ())), preferred_element_type=jnp.float32).astype(jnp.bfloat16)
    grad_inputs = lax.dot_general(grad_hidden, w_in, (((1,), (1,)), ((), ())), preferred_element_type=jnp.float32).astype(jnp.bfloat16)
    return (grad_inputs, grad_w_in, grad_w_out)
```

```python
import functools
import math

import jax
import jax.numpy as jnp
from jax import lax
from jax.experimental import pallas as pl
from jax.experimental.pallas import tpu as pltpu
from jax.sharding import PartitionSpec as P

N_X, N_Y, N_Z, N_C = 4, 4, 4, 2
TOK, WID, FFL = 512, 640, 5120
CHUNKS = (2560, 2560)
TILE = 512
AXES = ("row", "col")
F32, BF16 = jnp.float32, jnp.bfloat16


def neighbours(step, first):
    pairs = []
    for x in range(N_X):
        for y in range(N_Y):
            for z in range(N_Z):
                for c in range(N_C):
                    along_x = (c == 0) == first
                    nx = (x + step * along_x) % N_X
                    ny = (y + step * (not along_x)) % N_Y
                    here, there = ((a * N_Y + b) * N_Z + z for a, b in ((x, y), (nx, ny)))
                    pairs.append((here * N_C + c, there * N_C + c))
    return pairs


def hop(value, step, first):
    return lax.ppermute(value, AXES, neighbours(step, first))


def add(*terms):
    total = terms[0].astype(F32)
    for term in terms[1:]:
        total = total + term.astype(F32)
    return total


def gelu_parts(hidden):
    normal_cdf = 0.5 * (1.0 + jax.scipy.special.erf(hidden / math.sqrt(2.0)))
    density = jnp.exp(-0.5 * hidden * hidden) / math.sqrt(2.0 * math.pi)
    return (hidden * normal_cdf, normal_cdf + hidden * density)


def to_relative(order_ref, source_ref, target_ref):
    for block in range(16):
        start = pl.multiple_of(order_ref[block] * 32, 32)
        target_ref[block * 32 : (block + 1) * 32, :] = source_ref[pl.ds(start, 32), :]


def partial_kernel(order_ref, x_ref, c_ref, wi_ref, wo_ref, h2_ref, g2_ref, p1_ref, p3_ref, p0_ref, xs, cs):
    @pl.when(pl.program_id(0) == 0)
    def _():
        to_relative(order_ref, x_ref, xs)
        to_relative(order_ref, c_ref, cs)

    hidden = jnp.dot(xs[...], wi_ref[...], preferred_element_type=F32).astype(BF16)
    grad = lax.dot_general(
        cs[...], wo_ref[...], (((1,), (1,)), ((), ())), preferred_element_type=F32
    ).astype(BF16)
    p0_ref[0], p0_ref[1] = hidden[0:128], grad[0:128]
    p1_ref[0], p1_ref[1] = hidden[128:256], grad[128:256]
    h2_ref[...], g2_ref[...] = hidden[256:384], grad[256:384]
    p3_ref[0], p3_ref[1] = hidden[384:512], grad[384:512]


def partials(order, x_all, c_all, w_in, w_out, start, size):
    tiles, base = size // TILE, start // TILE
    pair = jax.ShapeDtypeStruct((2, 128, size), BF16)
    one = jax.ShapeDtypeStruct((128, size), BF16)
    pair_spec = pl.BlockSpec((2, 128, TILE), lambda i: (0, 0, i))
    one_spec = pl.BlockSpec((128, TILE), lambda i: (0, i))
    whole = pl.BlockSpec((TOK, WID), lambda i: (0, 0))
    return pl.pallas_call(
        partial_kernel,
        grid=(tiles,),
        out_shape=(one, one, pair, pair, pair),
        in_specs=[
            pl.BlockSpec(memory_space=pltpu.SMEM),
            whole,
            whole,
            pl.BlockSpec((WID, TILE), lambda i: (0, base + i)),
            pl.BlockSpec((TILE, WID), lambda i: (base + i, 0)),
        ],
        out_specs=(one_spec, one_spec, pair_spec, pair_spec, pair_spec),
        scratch_shapes=[pltpu.VMEM((TOK, WID), BF16), pltpu.VMEM((TOK, WID), BF16)],
        compiler_params=pltpu.CompilerParams(vmem_limit_bytes=32 * 2**20),
        cost_estimate=pl.CostEstimate(
            flops=4 * TOK * WID * size, bytes_accessed=4 * (TOK + WID) * size, transcendentals=0
        ),
        name="partials",
    )(order, x_all, c_all, w_in, w_out)


def grads_kernel(last, order_ref, x_ref, c_ref, wi_ref, o0_ref, o1_ref, o3_ref, a2_ref, b2_ref, *rest):
    gi_ref, gwi_ref, gwo_ref, xt, cs, total = rest[-6:]
    tile = pl.program_id(0)

    @pl.when(tile == 0)
    def _():
        to_relative(order_ref, c_ref, cs)
        to_relative(order_ref, x_ref, xt)
        total[...] = rest[0][...] if len(rest) > 6 else jnp.zeros_like(total)

    act = jnp.concatenate([o0_ref[0], o1_ref[0], a2_ref[...], o3_ref[0]], axis=0)
    grad = jnp.concatenate([o0_ref[1], o1_ref[1], b2_ref[...], o3_ref[1]], axis=0)
    total[...] += lax.dot_general(grad, wi_ref[...], (((1,), (1,)), ((), ())), preferred_element_type=F32)
    gwi_ref[...] = lax.dot_general(
        xt[...], grad, (((0,), (0,)), ((), ())), preferred_element_type=F32
    ).astype(BF16)
    gwo_ref[...] = lax.dot_general(
        act, cs[...], (((0,), (0,)), ((), ())), preferred_element_type=F32
    ).astype(BF16)

    @pl.when(tile == pl.num_programs(0) - 1)
    def _():
        if last:
            for block in range(16):
                start = pl.multiple_of(order_ref[block] * 32, 32)
                gi_ref[pl.ds(start, 32), :] = total[block * 32 : (block + 1) * 32, :].astype(BF16)
        else:
            gi_ref[...] = total[...]


def grads(order, x_all, c_all, w_in, gathered, before, start, size, last):
    tiles, base = size // TILE, start // TILE
    o0, o1, o3, a2, b2 = gathered
    pair_spec = pl.BlockSpec((2, 128, TILE), lambda i: (0, 0, i))
    one_spec = pl.BlockSpec((128, TILE), lambda i: (0, i))
    whole = pl.BlockSpec((TOK, WID), lambda i: (0, 0))
    any_spec = pl.BlockSpec(memory_space=pl.ANY)
    return pl.pallas_call(
        functools.partial(grads_kernel, last),
        grid=(tiles,),
        out_shape=(
            jax.ShapeDtypeStruct((TOK, WID), BF16 if last else F32),
            jax.ShapeDtypeStruct((WID, FFL), BF16),
            jax.ShapeDtypeStruct((FFL, WID), BF16),
        ),
        in_specs=[
            pl.BlockSpec(memory_space=pltpu.SMEM),
            whole,
            whole,
            pl.BlockSpec((WID, TILE), lambda i: (0, base + i)),
            pair_spec,
            pair_spec,
            pair_spec,
            one_spec,
            one_spec,
        ]
        + [whole, any_spec, any_spec][: len(before)],
        out_specs=(
            whole,
            pl.BlockSpec((WID, TILE), lambda i: (0, base + i)),
            pl.BlockSpec((TILE, WID), lambda i: (base + i, 0)),
        ),
        scratch_shapes=[
            pltpu.VMEM((TOK, WID), BF16),
            pltpu.VMEM((TOK, WID), BF16),
            pltpu.VMEM((TOK, WID), F32),
        ],
        input_output_aliases={10: 1, 11: 2} if before else {},
        compiler_params=pltpu.CompilerParams(vmem_limit_bytes=40 * 2**20),
        cost_estimate=pl.CostEstimate(
            flops=6 * TOK * WID * size, bytes_accessed=(4 * TOK + 6 * WID) * size, transcendentals=0
        ),
        name="grads",
    )(order, x_all, c_all, w_in, o0, o1, o3, a2, b2, *before)


def reduce_ring(h2, g2, p1, p3, p0, first):
    from_left = hop(h2, 1, first)
    from_right = hop(g2, -1, first)
    right = jnp.stack([add(p1[0], from_left).astype(BF16), p1[1]])
    left = jnp.stack([p3[0], add(p3[1], from_right).astype(BF16)])
    return add(p0, hop(right, 1, first), hop(left, -1, first))


def gather_ring(own, first):
    from_left = hop(own, 1, first)
    from_right = hop(own, -1, first)
    act = hop(from_left[0], 1, first)
    grad = hop(from_right[1], -1, first)
    return own, from_right, act, grad, from_left


def shards(inputs, cotangent, w_in, w_out):
    row, col = lax.axis_index("row"), lax.axis_index("col")
    x, y, core = row // N_Y, row % N_Y, col % N_C
    o = jnp.arange(16, dtype=jnp.int32)
    ox = jnp.where(core == 0, o // 4, o % 4)
    oy = jnp.where(core == 0, o % 4, o // 4)
    order = ((x + ox) % N_X) * N_Y + (y + oy) % N_Y

    x_all = lax.all_gather(inputs, "col", axis=0, tiled=True)
    c_all = lax.all_gather(cotangent, "col", axis=0, tiled=True)

    gathered = []
    start = 0
    for size in CHUNKS:
        h2, g2, p1, p3, p0 = partials(order, x_all, c_all, w_in, w_out, start, size)
        q = reduce_ring(h2, g2, p1, p3, p0, True).astype(BF16)
        b = [q[:, 32 * i : 32 * (i + 1)] for i in range(4)]
        hidden, grad_act = reduce_ring(b[2][0], b[2][1], b[1], b[3], b[0], False)
        activated, derivative = gelu_parts(hidden)
        own = jnp.stack([activated.astype(BF16), (grad_act * derivative).astype(BF16)])
        b0, b1, act, grad, b3 = gather_ring(own, False)
        quarter = jnp.concatenate([b0, b1, jnp.stack([act, grad]), b3], axis=1)
        o0, o1, act, grad, o3 = gather_ring(quarter, True)
        gathered.append((o0, o1, o3, act, grad))
        start += size

    before = ()
    start = 0
    for i, size in enumerate(CHUNKS):
        before = grads(
            order, x_all, c_all, w_in, gathered[i], before, start, size, i == len(CHUNKS) - 1
        )
        start += size
    gi, gwi, gwo = before
    parts = lax.all_to_all(gi.reshape(8, 64, WID), "col", 0, 0)
    gi = jnp.sum(parts.astype(F32), axis=0).astype(BF16)
    return gi, gwi, gwo


def solution(mesh):
    in_specs = (P("col", "row"), P("col", "row"), P("row", "col"), P("col", "row"))
    out_specs = (P("col", "row"), P("row", "col"), P("col", "row"))
    return jax.shard_map(shards, mesh=mesh, in_specs=in_specs, out_specs=out_specs, check_vma=False)
```

```python
import functools
import math

import jax
import jax.numpy as jnp
from jax import lax
from jax.experimental import pallas as pl
from jax.experimental.pallas import tpu as pltpu
from jax.sharding import PartitionSpec as P

N_X, N_Y, N_Z, N_C = 4, 4, 4, 2
TOK, WID, FFL = 512, 640, 5120
HALF = FFL // 2
TILE = 1280
TILES = FFL // TILE
AXES = ("row", "col")
F32, BF16 = jnp.float32, jnp.bfloat16
LIMIT = 24 * 2**20
STEPS = (
    ("h", "gather_z"),
    ("g", "gather_z"),
    ("h", "gather_core"),
    ("h", "partials"),
    ("g", "gather_core"),
    ("h", "send_far"),
    ("g", "partials"),
    ("h", "send_near"),
    ("g", "send_far"),
    ("g", "send_near"),
    ("h", "send_second"),
    ("g", "send_second"),
    ("h", "sum_second"),
    ("g", "sum_second"),
    ("", "activate"),
    ("g", "gather_near"),
    ("h", "gather_near"),
    ("g", "gather_far"),
    ("", "near_input_grads"),
    ("h", "gather_far"),
    ("", "far_input_grads"),
    ("", "grad_w_out"),
    ("", "sum_cores"),
    ("", "grad_w_in"),
    ("", "sum_z"),
)


def neighbours(move):
    pairs = []
    for x in range(N_X):
        for y in range(N_Y):
            for z in range(N_Z):
                for c in range(N_C):
                    nx, ny, nz, nc = move(x, y, z, c)
                    here = ((x * N_Y + y) * N_Z + z) * N_C + c
                    there = (((nx % N_X) * N_Y + ny % N_Y) * N_Z + nz % N_Z) * N_C + nc % N_C
                    pairs.append((here, there))
    return pairs


def hop(value, step, first):
    def move(x, y, z, c):
        return (x + step, y, z, c) if (c == 0) == first else (x, y + step, z, c)

    return lax.ppermute(value, AXES, neighbours(move))


def hop_z(value, step):
    return lax.ppermute(value, AXES, neighbours(lambda x, y, z, c: (x, y, z + step, c)))


def swap_core(value):
    return lax.ppermute(value, AXES, neighbours(lambda x, y, z, c: (x, y, z, c + 1)))


def add(*terms):
    total = terms[0].astype(F32)
    for term in terms[1:]:
        total = total + term.astype(F32)
    return total


def gelu_parts(hidden):
    normal_cdf = 0.5 * (1.0 + jax.scipy.special.erf(hidden / math.sqrt(2.0)))
    density = jnp.exp(-0.5 * hidden * hidden) / math.sqrt(2.0 * math.pi)
    return (hidden * normal_cdf, normal_cdf + hidden * density)


def store_partials(term, far_left_ref, far_right_ref, p1_ref, p3_ref, p0_ref):
    tile = pl.program_id(0)
    p0_ref[...] = term[0:128]
    p1_ref[...] = term[128:256]
    p3_ref[...] = term[384:512]

    @pl.when(tile < TILES // 2)
    def _():
        far_left_ref[...] = term[256:384]

    @pl.when(tile >= TILES // 2)
    def _():
        far_right_ref[...] = term[256:384]


def partial_kernel(hidden, order_ref, all_ref, w_ref, rows_ref, *outs):
    @pl.when(pl.program_id(0) == 0)
    def _():
        for block in range(16):
            start = pl.multiple_of(order_ref[block] * 32, 32)
            rows_ref[block * 32 : (block + 1) * 32, :] = all_ref[pl.ds(start, 32), :]

    sides = (((1,), (0 if hidden else 1,)), ((), ()))
    term = lax.dot_general(rows_ref[...], w_ref[...], sides, preferred_element_type=F32)
    store_partials(term.astype(BF16), *outs)


def partials(hidden, order, tokens, weight):
    whole = pl.BlockSpec((TOK, WID), lambda i: (0, 0))
    rows = jax.ShapeDtypeStruct((TOK, WID), BF16)
    half = jax.ShapeDtypeStruct((128, HALF), BF16)
    block = jax.ShapeDtypeStruct((128, FFL), BF16)
    spec = pl.BlockSpec((128, TILE), lambda i: (0, i))
    left = pl.BlockSpec((128, TILE), lambda i: (0, jnp.minimum(i, TILES // 2 - 1)))
    right = pl.BlockSpec((128, TILE), lambda i: (0, jnp.maximum(i - TILES // 2, 0)))
    return pl.pallas_call(
        functools.partial(partial_kernel, hidden),
        grid=(TILES,),
        out_shape=(rows, half, half, block, block, block),
        in_specs=[
            pl.BlockSpec(memory_space=pltpu.SMEM),
            whole,
            pl.BlockSpec((WID, TILE), lambda i: (0, i))
            if hidden
            else pl.BlockSpec((TILE, WID), lambda i: (i, 0)),
        ],
        out_specs=(whole, left, right, spec, spec, spec),
        compiler_params=pltpu.CompilerParams(vmem_limit_bytes=LIMIT),
        cost_estimate=pl.CostEstimate(
            flops=2 * TOK * WID * FFL, bytes_accessed=2 * (TOK + WID) * FFL, transcendentals=0
        ),
        name="hidden_partials" if hidden else "grad_partials",
    )(order, tokens, weight)


def near_input_grads_kernel(wi_ref, b0_ref, b1_ref, b3_ref, out_ref):
    @pl.when(pl.program_id(0) == 0)
    def _():
        out_ref[...] = jnp.zeros_like(out_ref)

    grad = jnp.concatenate([b0_ref[...], b1_ref[...], b3_ref[...]], axis=0)
    out_ref[...] += lax.dot_general(grad, wi_ref[...], (((1,), (1,)), ((), ())), preferred_element_type=F32)


def far_input_grads_kernel(order_ref, wi_ref, b2_ref, near_ref, out_ref, total):
    @pl.when(pl.program_id(0) == 0)
    def _():
        total[...] = jnp.zeros_like(total)

    total[...] += lax.dot_general(
        b2_ref[...], wi_ref[...], (((1,), (1,)), ((), ())), preferred_element_type=F32
    )

    @pl.when(pl.program_id(0) == pl.num_programs(0) - 1)
    def _():
        for block in range(16):
            rows = pl.ds(pl.multiple_of(order_ref[block] * 32, 32), 32)
            low = (block % 4) * 32
            if block // 4 == 2:
                term = total[low : low + 32, :]
            else:
                low += (0, 128, 0, 256)[block // 4]
                term = near_ref[low : low + 32, :]
            out_ref[rows, :] = term.astype(BF16)


def input_grads(w_in, blocks, near=None, order=None):
    last = near is not None
    whole = lambda rows: pl.BlockSpec((rows, WID), lambda i: (0, 0))
    return pl.pallas_call(
        far_input_grads_kernel if last else near_input_grads_kernel,
        grid=(TILES,),
        out_shape=jax.ShapeDtypeStruct((TOK, WID), BF16) if last else jax.ShapeDtypeStruct((384, WID), F32),
        in_specs=([pl.BlockSpec(memory_space=pltpu.SMEM)] if last else [])
        + [pl.BlockSpec((WID, TILE), lambda i: (0, i))]
        + [pl.BlockSpec((128, TILE), lambda i: (0, i)) for _ in blocks]
        + ([whole(384)] if last else []),
        out_specs=whole(TOK if last else 384),
        scratch_shapes=[pltpu.VMEM((128, WID), F32)] if last else [],
        compiler_params=pltpu.CompilerParams(vmem_limit_bytes=LIMIT),
        cost_estimate=pl.CostEstimate(
            flops=2 * 128 * len(blocks) * WID * FFL, bytes_accessed=2 * (TOK + WID) * FFL, transcendentals=0
        ),
        name="far_input_grads" if last else "near_input_grads",
    )(*((order,) if last else ()), w_in, *blocks, *((near,) if last else ()))


def w_out_kernel(c_ref, b0_ref, b1_ref, b2_ref, b3_ref, out_ref):
    act = jnp.concatenate([b0_ref[...], b1_ref[...], b2_ref[...], b3_ref[...]], axis=0)
    out_ref[...] = lax.dot_general(
        act, c_ref[...], (((0,), (0,)), ((), ())), preferred_element_type=F32
    ).astype(BF16)


def w_in_kernel(x_ref, b0_ref, b1_ref, b2_ref, b3_ref, out_ref):
    grad = jnp.concatenate([b0_ref[...], b1_ref[...], b2_ref[...], b3_ref[...]], axis=0)
    out_ref[...] = lax.dot_general(
        x_ref[...], grad, (((0,), (0,)), ((), ())), preferred_element_type=F32
    ).astype(BF16)


def weight_grads(outer, rows, blocks):
    return pl.pallas_call(
        w_out_kernel if outer else w_in_kernel,
        grid=(TILES,),
        out_shape=jax.ShapeDtypeStruct((FFL, WID) if outer else (WID, FFL), BF16),
        in_specs=[pl.BlockSpec((TOK, WID), lambda i: (0, 0))]
        + [pl.BlockSpec((128, TILE), lambda i: (0, i))] * 4,
        out_specs=(
            pl.BlockSpec((TILE, WID), lambda i: (i, 0))
            if outer
            else pl.BlockSpec((WID, TILE), lambda i: (0, i))
        ),
        compiler_params=pltpu.CompilerParams(vmem_limit_bytes=LIMIT),
        cost_estimate=pl.CostEstimate(
            flops=2 * TOK * WID, bytes_accessed=2 * (TOK + WID), transcendentals=0
        ),
        name="grad_w_out" if outer else "grad_w_in",
    )(rows, *blocks)


class Stream:
    def __init__(self, hidden, tokens, weight):
        self.hidden, self.own, self.weight = hidden, tokens, weight

    def gather_z(self, env):
        self.came = tuple(hop_z(self.own, step) for step in (2, 1, -1))
        return ()

    def gather_core(self, env):
        far, left, right = env.after(self.came)
        self.own = jnp.concatenate([self.own, right, far, left], axis=0)
        self.came = swap_core(self.own)
        return (self.own,)

    def partials(self, env):
        tokens = jnp.concatenate([self.own, env.after(self.came)], axis=0)
        self.rows, *parts = partials(self.hidden, env.order, tokens, self.weight)
        self.far_left, self.far_right, self.p1, self.p3, self.p0 = parts
        return parts

    def send_far(self, env):
        left, right = env.after((self.far_left, self.far_right))
        self.came = hop(left, 1, True), hop(right, -1, True)

    def send_near(self, env):
        from_left, from_right = env.after(self.came)
        right = jnp.concatenate([add(self.p1[:, :HALF], from_left).astype(BF16), self.p1[:, HALF:]], axis=1)
        left = jnp.concatenate([self.p3[:, :HALF], add(self.p3[:, HALF:], from_right).astype(BF16)], axis=1)
        self.came = hop(right, 1, True), hop(left, -1, True)
        return right, left

    def send_second(self, env):
        from_left, from_right = env.after(self.came)
        q = add(self.p0, from_left, from_right).astype(BF16)
        blocks = [q[32 * i : 32 * (i + 1)] for i in range(4)]
        self.own = blocks[0]
        self.came = tuple(hop(blocks[i], step, False) for i, step in ((2, 2), (1, 1), (3, -1)))
        return (q,)

    def sum_second(self, env):
        self.own = add(self.own, *env.after(self.came))
        return (self.own,)

    def send_own(self):
        self.came = tuple(hop(self.own, step, False) for step in (2, 1, -1))

    def gather_near(self, env):
        far, left, right = env.after(self.came)
        self.quarter = jnp.concatenate([self.own, right, far, left], axis=0)
        self.came = hop(self.quarter, 1, True), hop(self.quarter, -1, True)
        return (self.quarter,)

    def gather_far(self, env):
        self.left, self.right = env.after(self.came)
        halves = self.left[:, :HALF], self.right[:, HALF:]
        self.came = hop(halves[0], 1, True), hop(halves[1], -1, True)
        return halves

    def blocks(self, env):
        far = jnp.concatenate(env.after(self.came), axis=1)
        return self.quarter, self.right, far, self.left


class Env:
    def __init__(self, **given):
        self.__dict__.update(given)
        self.last = ()

    def after(self, values):
        return lax.optimization_barrier((values, self.last))[0] if self.last else values

    def activate(self, env):
        activated, derivative = gelu_parts(self.h.own)
        self.h.own, self.g.own = activated.astype(BF16), (self.g.own * derivative).astype(BF16)
        self.g.send_own()
        self.h.send_own()
        return self.g.own, self.h.own

    def near_input_grads(self, env):
        g = self.g
        self.near = input_grads(self.w_in, env.after((g.quarter, g.right, g.left)))
        return (self.near,)

    def far_input_grads(self, env):
        self.grad_blocks = self.g.blocks(env)
        sums = input_grads(self.w_in, self.grad_blocks[2:3], self.near, self.order)
        self.sums = sums.reshape(2, N_Z, 64, WID)
        self.swapped = swap_core(self.sums[1])
        return (self.sums,)

    def grad_w_in(self, env):
        self.w_in_result = weight_grads(False, env.after(self.h.rows), self.grad_blocks)
        return (self.w_in_result,)

    def sum_cores(self, env):
        total = add(self.sums[0], env.after(self.swapped)).astype(BF16)
        self.kept = total[0]
        self.crossed = tuple(hop_z(total[step % N_Z], step) for step in (2, 1, -1))
        return (total,)

    def grad_w_out(self, env):
        self.w_out_result = weight_grads(True, self.g.rows, self.h.blocks(env))
        return (self.w_out_result,)

    def sum_z(self, env):
        self.inputs_result = add(self.kept, *env.after(self.crossed)).astype(BF16)
        return (self.inputs_result,)


def shards(inputs, cotangent, w_in, w_out):
    row, col = lax.axis_index("row"), lax.axis_index("col")
    x, y, z, core = row // N_Y, row % N_Y, col // N_C, col % N_C
    o = jnp.arange(16, dtype=jnp.int32)
    ox = jnp.where(core == 0, o // 4, o % 4)
    oy = jnp.where(core == 0, o % 4, o // 4)
    block = ((x + ox) % N_X) * N_Y + (y + oy) % N_Y
    other = (block // 2 + core) % N_C
    order = (other * N_Z + (block // 4 - z) % N_Z) * 2 + block % 2

    env = Env(order=order, w_in=w_in, h=Stream(True, inputs, w_in), g=Stream(False, cotangent, w_out))
    for where, step in STEPS:
        env.last = getattr(getattr(env, where) if where else env, step)(env) or env.last
    return env.inputs_result, env.w_in_result, env.w_out_result


def solution(mesh):
    in_specs = (P("col", "row"), P("col", "row"), P("row", "col"), P("col", "row"))
    out_specs = (P("col", "row"), P("row", "col"), P("col", "row"))
    return jax.shard_map(shards, mesh=mesh, in_specs=in_specs, out_specs=out_specs, check_vma=False)
```

```python
import functools
import math

import jax
import jax.numpy as jnp
from jax import lax
from jax.experimental import pallas as pl
from jax.experimental.pallas import tpu as pltpu
from jax.sharding import PartitionSpec as P

N_X, N_Y, N_Z, N_C = 4, 4, 4, 2
TOK, WID, FFL = 512, 640, 5120
HALF = FFL // 2
TILE = 1280
TILES = FFL // TILE
AXES = ("row", "col")
F32, BF16 = jnp.float32, jnp.bfloat16
LIMIT = 24 * 2**20
STEPS = (
    ("h", "gather_z"),
    ("g", "gather_z"),
    ("h", "gather_core"),
    ("h", "partials"),
    ("g", "gather_core"),
    ("h", "send_far"),
    ("g", "partials"),
    ("g", "send_far"),
    ("h", "send_near"),
    ("g", "send_near"),
    ("h", "send_second"),
    ("g", "send_second"),
    ("h", "sum_second"),
    ("g", "sum_second"),
    ("", "activate"),
    ("g", "gather_near"),
    ("h", "gather_near"),
    ("g", "gather_far"),
    ("", "near_input_grads"),
    ("h", "gather_far"),
    ("", "far_input_grads"),
    ("", "grad_w_out"),
    ("", "sum_cores"),
    ("", "grad_w_in"),
    ("", "sum_z"),
)


def neighbours(move):
    pairs = []
    for x in range(N_X):
        for y in range(N_Y):
            for z in range(N_Z):
                for c in range(N_C):
                    nx, ny, nz, nc = move(x, y, z, c)
                    here = ((x * N_Y + y) * N_Z + z) * N_C + c
                    there = (((nx % N_X) * N_Y + ny % N_Y) * N_Z + nz % N_Z) * N_C + nc % N_C
                    pairs.append((here, there))
    return pairs


def hop(value, step, first):
    def move(x, y, z, c):
        return (x + step, y, z, c) if (c == 0) == first else (x, y + step, z, c)

    return lax.ppermute(value, AXES, neighbours(move))


def hop_z(value, step):
    return lax.ppermute(value, AXES, neighbours(lambda x, y, z, c: (x, y, z + step, c)))


def swap_core(value):
    return lax.ppermute(value, AXES, neighbours(lambda x, y, z, c: (x, y, z, c + 1)))


def add(*terms):
    total = terms[0].astype(F32)
    for term in terms[1:]:
        total = total + term.astype(F32)
    return total


def gelu_parts(hidden):
    normal_cdf = 0.5 * (1.0 + jax.scipy.special.erf(hidden / math.sqrt(2.0)))
    density = jnp.exp(-0.5 * hidden * hidden) / math.sqrt(2.0 * math.pi)
    return (hidden * normal_cdf, normal_cdf + hidden * density)


def store_partials(term, far_left_ref, far_right_ref, p1_ref, p3_ref, p0_ref):
    tile = pl.program_id(0)
    p0_ref[...] = term[0:128]
    p1_ref[...] = term[128:256]
    p3_ref[...] = term[384:512]

    @pl.when(tile < TILES // 2)
    def _():
        far_left_ref[...] = term[256:384]

    @pl.when(tile >= TILES // 2)
    def _():
        far_right_ref[...] = term[256:384]


def partial_kernel(hidden, order_ref, all_ref, w_ref, rows_ref, *outs):
    @pl.when(pl.program_id(0) == 0)
    def _():
        for block in range(16):
            start = pl.multiple_of(order_ref[block] * 32, 32)
            rows_ref[block * 32 : (block + 1) * 32, :] = all_ref[pl.ds(start, 32), :]

    sides = (((1,), (0 if hidden else 1,)), ((), ()))
    term = lax.dot_general(rows_ref[...], w_ref[...], sides, preferred_element_type=F32)
    store_partials(term.astype(BF16), *outs)


def partials(hidden, order, tokens, weight):
    whole = pl.BlockSpec((TOK, WID), lambda i: (0, 0))
    rows = jax.ShapeDtypeStruct((TOK, WID), BF16)
    half = jax.ShapeDtypeStruct((128, HALF), BF16)
    block = jax.ShapeDtypeStruct((128, FFL), BF16)
    spec = pl.BlockSpec((128, TILE), lambda i: (0, i))
    left = pl.BlockSpec((128, TILE), lambda i: (0, jnp.minimum(i, TILES // 2 - 1)))
    right = pl.BlockSpec((128, TILE), lambda i: (0, jnp.maximum(i - TILES // 2, 0)))
    return pl.pallas_call(
        functools.partial(partial_kernel, hidden),
        grid=(TILES,),
        out_shape=(rows, half, half, block, block, block),
        in_specs=[
            pl.BlockSpec(memory_space=pltpu.SMEM),
            whole,
            pl.BlockSpec((WID, TILE), lambda i: (0, i))
            if hidden
            else pl.BlockSpec((TILE, WID), lambda i: (i, 0)),
        ],
        out_specs=(whole, left, right, spec, spec, spec),
        compiler_params=pltpu.CompilerParams(vmem_limit_bytes=LIMIT),
        cost_estimate=pl.CostEstimate(
            flops=2 * TOK * WID * FFL, bytes_accessed=2 * (TOK + WID) * FFL, transcendentals=0
        ),
        name="hidden_partials" if hidden else "grad_partials",
    )(order, tokens, weight)


def stage_kernel(source_ref, target_ref):
    target_ref[...] = source_ref[...]


def stage(rows):
    return pl.pallas_call(
        stage_kernel,
        out_shape=jax.ShapeDtypeStruct(rows.shape, rows.dtype),
        compiler_params=pltpu.CompilerParams(vmem_limit_bytes=LIMIT),
        cost_estimate=pl.CostEstimate(
            flops=4 * TOK * WID * FFL, bytes_accessed=4 * WID * FFL, transcendentals=0
        ),
        name="stage",
    )(rows)


def near_input_grads_kernel(wi_ref, b0_ref, b1_ref, b3_ref, out_ref):
    @pl.when(pl.program_id(0) == 0)
    def _():
        out_ref[...] = jnp.zeros_like(out_ref)

    grad = jnp.concatenate([b0_ref[...], b1_ref[...], b3_ref[...]], axis=0)
    out_ref[...] += lax.dot_general(grad, wi_ref[...], (((1,), (1,)), ((), ())), preferred_element_type=F32)


def far_input_grads_kernel(order_ref, wi_ref, b2_ref, near_ref, out_ref, total):
    @pl.when(pl.program_id(0) == 0)
    def _():
        total[...] = jnp.zeros_like(total)

    total[...] += lax.dot_general(
        b2_ref[...], wi_ref[...], (((1,), (1,)), ((), ())), preferred_element_type=F32
    )

    @pl.when(pl.program_id(0) == pl.num_programs(0) - 1)
    def _():
        for block in range(16):
            rows = pl.ds(pl.multiple_of(order_ref[block] * 32, 32), 32)
            low = (block % 4) * 32
            if block // 4 == 2:
                term = total[low : low + 32, :]
            else:
                low += (0, 128, 0, 256)[block // 4]
                term = near_ref[low : low + 32, :]
            out_ref[rows, :] = term.astype(BF16)


def input_grads(w_in, blocks, near=None, order=None):
    last = near is not None
    whole = lambda rows: pl.BlockSpec((rows, WID), lambda i: (0, 0))
    return pl.pallas_call(
        far_input_grads_kernel if last else near_input_grads_kernel,
        grid=(TILES,),
        out_shape=jax.ShapeDtypeStruct((TOK, WID), BF16) if last else jax.ShapeDtypeStruct((384, WID), F32),
        in_specs=([pl.BlockSpec(memory_space=pltpu.SMEM)] if last else [])
        + [pl.BlockSpec((WID, TILE), lambda i: (0, i))]
        + [pl.BlockSpec((128, TILE), lambda i: (0, i)) for _ in blocks]
        + ([whole(384)] if last else []),
        out_specs=whole(TOK if last else 384),
        scratch_shapes=[pltpu.VMEM((128, WID), F32)] if last else [],
        compiler_params=pltpu.CompilerParams(vmem_limit_bytes=LIMIT),
        cost_estimate=pl.CostEstimate(
            flops=2 * 128 * len(blocks) * WID * FFL, bytes_accessed=2 * (TOK + WID) * FFL, transcendentals=0
        ),
        name="far_input_grads" if last else "near_input_grads",
    )(*((order,) if last else ()), w_in, *blocks, *((near,) if last else ()))


def w_out_kernel(c_ref, b0_ref, b1_ref, b2_ref, b3_ref, out_ref):
    act = jnp.concatenate([b0_ref[...], b1_ref[...], b2_ref[...], b3_ref[...]], axis=0)
    out_ref[...] = lax.dot_general(
        act, c_ref[...], (((0,), (0,)), ((), ())), preferred_element_type=F32
    ).astype(BF16)


def w_in_kernel(x_ref, b0_ref, b1_ref, b2_ref, b3_ref, out_ref):
    grad = jnp.concatenate([b0_ref[...], b1_ref[...], b2_ref[...], b3_ref[...]], axis=0)
    out_ref[...] = lax.dot_general(
        x_ref[...], grad, (((0,), (0,)), ((), ())), preferred_element_type=F32
    ).astype(BF16)


def weight_grads(outer, rows, blocks):
    return pl.pallas_call(
        w_out_kernel if outer else w_in_kernel,
        grid=(TILES,),
        out_shape=jax.ShapeDtypeStruct((FFL, WID) if outer else (WID, FFL), BF16),
        in_specs=[pl.BlockSpec((TOK, WID), lambda i: (0, 0))]
        + [pl.BlockSpec((128, TILE), lambda i: (0, i))] * 4,
        out_specs=(
            pl.BlockSpec((TILE, WID), lambda i: (i, 0))
            if outer
            else pl.BlockSpec((WID, TILE), lambda i: (0, i))
        ),
        compiler_params=pltpu.CompilerParams(vmem_limit_bytes=LIMIT),
        cost_estimate=pl.CostEstimate(
            flops=2 * TOK * WID, bytes_accessed=2 * (TOK + WID), transcendentals=0
        ),
        name="grad_w_out" if outer else "grad_w_in",
    )(rows, *blocks)


class Stream:
    def __init__(self, hidden, tokens, weight):
        self.hidden, self.own, self.weight = hidden, tokens, weight

    def gather_z(self, env):
        self.came = tuple(hop_z(self.own, step) for step in (2, 1, -1))
        return ()

    def gather_core(self, env):
        own, far, left, right = env.after((self.own, *self.came))
        own = jnp.concatenate([own, right, far, left], axis=0)
        self.came = swap_core(own)
        self.own = stage(own) if self.hidden else own
        return (self.own,)

    def partials(self, env):
        tokens = jnp.concatenate([self.own, env.after(self.came)], axis=0)
        self.rows, *parts = partials(self.hidden, env.order, tokens, self.weight)
        self.far_left, self.far_right, self.p1, self.p3, self.p0 = parts
        return parts

    def send_far(self, env):
        left, right = env.after((self.far_left, self.far_right))
        self.came = hop(left, 1, True), hop(right, -1, True)

    def send_near(self, env):
        from_left, from_right = env.after(self.came)
        right = jnp.concatenate([add(self.p1[:, :HALF], from_left).astype(BF16), self.p1[:, HALF:]], axis=1)
        left = jnp.concatenate([self.p3[:, :HALF], add(self.p3[:, HALF:], from_right).astype(BF16)], axis=1)
        self.came = hop(right, 1, True), hop(left, -1, True)
        return right, left

    def send_second(self, env):
        from_left, from_right = env.after(self.came)
        q = add(self.p0, from_left, from_right).astype(BF16)
        blocks = [q[32 * i : 32 * (i + 1)] for i in range(4)]
        self.own = blocks[0]
        self.came = tuple(hop(blocks[i], step, False) for i, step in ((3, -1), (1, 1), (2, 2)))
        return (q,)

    def sum_second(self, env):
        self.own = add(self.own, *env.after(self.came))
        return (self.own,)

    def send_own(self):
        self.came = tuple(hop(self.own, step, False) for step in (-1, 1, 2))

    def gather_near(self, env):
        right, left, far = env.after(self.came)
        self.quarter = jnp.concatenate([self.own, right, far, left], axis=0)
        self.came = hop(self.quarter, 1, True), hop(self.quarter, -1, True)
        return (self.quarter,)

    def gather_far(self, env):
        self.left, self.right = env.after(self.came)
        halves = self.left[:, :HALF], self.right[:, HALF:]
        self.came = hop(halves[0], 1, True), hop(halves[1], -1, True)
        return halves

    def blocks(self, env):
        far = jnp.concatenate(env.after(self.came), axis=1)
        return self.quarter, self.right, far, self.left


class Env:
    def __init__(self, **given):
        self.__dict__.update(given)
        self.last = ()

    def after(self, values):
        return lax.optimization_barrier((values, self.last))[0] if self.last else values

    def activate(self, env):
        activated, derivative = gelu_parts(self.h.own)
        self.h.own, self.g.own = activated.astype(BF16), (self.g.own * derivative).astype(BF16)
        self.g.send_own()
        self.h.send_own()
        return self.g.own, self.h.own

    def near_input_grads(self, env):
        g = self.g
        self.near = input_grads(self.w_in, env.after((g.quarter, g.right, g.left)))
        return (self.near,)

    def far_input_grads(self, env):
        self.grad_blocks = self.g.blocks(env)
        sums = input_grads(self.w_in, self.grad_blocks[2:3], self.near, self.order)
        self.sums = sums.reshape(2, N_Z, 64, WID)
        self.swapped = swap_core(self.sums[1])
        return (self.sums,)

    def grad_w_in(self, env):
        self.w_in_result = weight_grads(False, env.after(self.h.rows), self.grad_blocks)
        return (self.w_in_result,)

    def sum_cores(self, env):
        total = add(self.sums[0], env.after(self.swapped)).astype(BF16)
        self.kept = total[0]
        self.crossed = tuple(hop_z(total[step % N_Z], step) for step in (2, 1, -1))
        return (total,)

    def grad_w_out(self, env):
        self.w_out_result = weight_grads(True, self.g.rows, self.h.blocks(env))
        return (self.w_out_result,)

    def sum_z(self, env):
        self.inputs_result = add(self.kept, *env.after(self.crossed)).astype(BF16)
        return (self.inputs_result,)


def shards(inputs, cotangent, w_in, w_out):
    row, col = lax.axis_index("row"), lax.axis_index("col")
    x, y, z, core = row // N_Y, row % N_Y, col // N_C, col % N_C
    o = jnp.arange(16, dtype=jnp.int32)
    ox = jnp.where(core == 0, o // 4, o % 4)
    oy = jnp.where(core == 0, o % 4, o // 4)
    block = ((x + ox) % N_X) * N_Y + (y + oy) % N_Y
    other = (block // 2 + core) % N_C
    order = (other * N_Z + (block // 4 - z) % N_Z) * 2 + block % 2

    env = Env(order=order, w_in=w_in, h=Stream(True, inputs, w_in), g=Stream(False, cotangent, w_out))
    for where, step in STEPS:
        env.last = getattr(getattr(env, where) if where else env, step)(env) or env.last
    return env.inputs_result, env.w_in_result, env.w_out_result


def solution(mesh):
    in_specs = (P("col", "row"), P("col", "row"), P("row", "col"), P("col", "row"))
    out_specs = (P("col", "row"), P("row", "col"), P("col", "row"))
    return jax.shard_map(shards, mesh=mesh, in_specs=in_specs, out_specs=out_specs, check_vma=False)
```

```python
import functools
import math

import jax
import jax.numpy as jnp
from jax import lax
from jax.experimental import pallas as pl
from jax.experimental.pallas import tpu as pltpu
from jax.sharding import PartitionSpec as P

N_X, N_Y, N_Z, N_C = 4, 4, 4, 2
TOK, WID, FFL = 512, 640, 5120
HALF = FFL // 2
TILE = 2560
TILES = FFL // TILE
AXES = ("row", "col")
F32, BF16 = jnp.float32, jnp.bfloat16
LIMIT = 32 * 2**20
STEPS = (
    ("h", "gather_z"),
    ("g", "gather_z"),
    ("h", "gather_core"),
    ("g", "gather_z_far"),
    ("h", "partials"),
    ("g", "gather_core"),
    ("h", "send_far"),
    ("g", "partials"),
    ("g", "send_far"),
    ("h", "send_near"),
    ("g", "send_near"),
    ("h", "send_second"),
    ("g", "send_second"),
    ("h", "sum_second"),
    ("g", "sum_second"),
    ("", "activate"),
    ("g", "gather_near"),
    ("h", "gather_near"),
    ("g", "gather_far"),
    ("", "near_input_grads"),
    ("", "near_grad_w_in"),
    ("h", "gather_far"),
    ("", "near_grad_w_out"),
    ("", "far_input_grads"),
    ("", "grad_w_out"),
    ("", "sum_cores"),
    ("", "grad_w_in"),
    ("", "sum_z"),
)


def neighbours(move):
    pairs = []
    for x in range(N_X):
        for y in range(N_Y):
            for z in range(N_Z):
                for c in range(N_C):
                    nx, ny, nz, nc = move(x, y, z, c)
                    here = ((x * N_Y + y) * N_Z + z) * N_C + c
                    there = (((nx % N_X) * N_Y + ny % N_Y) * N_Z + nz % N_Z) * N_C + nc % N_C
                    pairs.append((here, there))
    return pairs


def hop(value, step, first):
    def move(x, y, z, c):
        return (x + step, y, z, c) if (c == 0) == first else (x, y + step, z, c)

    return lax.ppermute(value, AXES, neighbours(move))


def hop_z(value, step):
    return lax.ppermute(value, AXES, neighbours(lambda x, y, z, c: (x, y, z + step, c)))


def swap_core(value):
    return lax.ppermute(value, AXES, neighbours(lambda x, y, z, c: (x, y, z, c + 1)))


def add(*terms):
    total = terms[0].astype(F32)
    for term in terms[1:]:
        total = total + term.astype(F32)
    return total


def gelu_parts(hidden):
    normal_cdf = 0.5 * (1.0 + jax.scipy.special.erf(hidden / math.sqrt(2.0)))
    density = jnp.exp(-0.5 * hidden * hidden) / math.sqrt(2.0 * math.pi)
    return (hidden * normal_cdf, normal_cdf + hidden * density)


def store_partials(term, far_left_ref, far_right_ref, p1_ref, p3_ref, p0_ref):
    tile = pl.program_id(0)
    p0_ref[...] = term[0:128]
    p1_ref[...] = term[128:256]
    p3_ref[...] = term[384:512]

    @pl.when(tile < TILES // 2)
    def _():
        far_left_ref[...] = term[256:384]

    @pl.when(tile >= TILES // 2)
    def _():
        far_right_ref[...] = term[256:384]


def partial_kernel(hidden, order_ref, all_ref, w_ref, rows_ref, *outs):
    @pl.when(pl.program_id(0) == 0)
    def _():
        for block in range(16):
            start = pl.multiple_of(order_ref[block] * 32, 32)
            rows_ref[block * 32 : (block + 1) * 32, :] = all_ref[pl.ds(start, 32), :]

    sides = (((1,), (0 if hidden else 1,)), ((), ()))
    term = lax.dot_general(rows_ref[...], w_ref[...], sides, preferred_element_type=F32)
    store_partials(term.astype(BF16), *outs)


def partials(hidden, order, tokens, weight):
    whole = pl.BlockSpec((TOK, WID), lambda i: (0, 0))
    rows = jax.ShapeDtypeStruct((TOK, WID), BF16)
    half = jax.ShapeDtypeStruct((128, HALF), BF16)
    block = jax.ShapeDtypeStruct((128, FFL), BF16)
    spec = pl.BlockSpec((128, TILE), lambda i: (0, i))
    left = pl.BlockSpec((128, TILE), lambda i: (0, jnp.minimum(i, TILES // 2 - 1)))
    right = pl.BlockSpec((128, TILE), lambda i: (0, jnp.maximum(i - TILES // 2, 0)))
    return pl.pallas_call(
        functools.partial(partial_kernel, hidden),
        grid=(TILES,),
        out_shape=(rows, half, half, block, block, block),
        in_specs=[
            pl.BlockSpec(memory_space=pltpu.SMEM),
            whole,
            pl.BlockSpec((WID, TILE), lambda i: (0, i))
            if hidden
            else pl.BlockSpec((TILE, WID), lambda i: (i, 0)),
        ],
        out_specs=(whole, left, right, spec, spec, spec),
        compiler_params=pltpu.CompilerParams(vmem_limit_bytes=LIMIT),
        cost_estimate=pl.CostEstimate(
            flops=2 * TOK * WID * FFL, bytes_accessed=2 * (TOK + WID) * FFL, transcendentals=0
        ),
        name="hidden_partials" if hidden else "grad_partials",
    )(order, tokens, weight)


def stage_kernel(source_ref, target_ref):
    target_ref[...] = source_ref[...]


def stage(rows):
    return pl.pallas_call(
        stage_kernel,
        out_shape=jax.ShapeDtypeStruct(rows.shape, rows.dtype),
        compiler_params=pltpu.CompilerParams(vmem_limit_bytes=LIMIT),
        cost_estimate=pl.CostEstimate(
            flops=4 * TOK * WID * FFL, bytes_accessed=4 * WID * FFL, transcendentals=0
        ),
        name="stage",
    )(rows)


def near_input_grads_kernel(wi_ref, b0_ref, b1_ref, b3_ref, out_ref):
    @pl.when(pl.program_id(0) == 0)
    def _():
        out_ref[...] = jnp.zeros_like(out_ref)

    grad = jnp.concatenate([b0_ref[...], b1_ref[...], b3_ref[...]], axis=0)
    out_ref[...] += lax.dot_general(grad, wi_ref[...], (((1,), (1,)), ((), ())), preferred_element_type=F32)


def chosen(left_ref, right_ref):
    return jnp.where(pl.program_id(0) < TILES // 2, left_ref[...], right_ref[...])


def far_input_grads_kernel(order_ref, wi_ref, left_ref, right_ref, near_ref, out_ref, total):
    @pl.when(pl.program_id(0) == 0)
    def _():
        total[...] = jnp.zeros_like(total)

    total[...] += lax.dot_general(
        chosen(left_ref, right_ref), wi_ref[...], (((1,), (1,)), ((), ())), preferred_element_type=F32
    )

    @pl.when(pl.program_id(0) == pl.num_programs(0) - 1)
    def _():
        for block in range(16):
            rows = pl.ds(pl.multiple_of(order_ref[block] * 32, 32), 32)
            low = (block % 4) * 32
            if block // 4 == 2:
                term = total[low : low + 32, :]
            else:
                low += (0, 128, 0, 256)[block // 4]
                term = near_ref[low : low + 32, :]
            out_ref[rows, :] = term.astype(BF16)


def block_specs(last, blocks):
    if not last:
        return [pl.BlockSpec((128, TILE), lambda i: (0, i)) for _ in blocks]
    return [
        pl.BlockSpec((128, TILE), lambda i: (0, jnp.minimum(i, TILES // 2 - 1))),
        pl.BlockSpec((128, TILE), lambda i: (0, jnp.maximum(i - TILES // 2, 0))),
    ]


def input_grads(w_in, blocks, near=None, order=None):
    last = near is not None
    whole = lambda rows: pl.BlockSpec((rows, WID), lambda i: (0, 0))
    return pl.pallas_call(
        far_input_grads_kernel if last else near_input_grads_kernel,
        grid=(TILES,),
        out_shape=jax.ShapeDtypeStruct((TOK, WID), BF16) if last else jax.ShapeDtypeStruct((384, WID), F32),
        in_specs=([pl.BlockSpec(memory_space=pltpu.SMEM)] if last else [])
        + [pl.BlockSpec((WID, TILE), lambda i: (0, i))]
        + block_specs(last, blocks)
        + ([whole(384)] if last else []),
        out_specs=whole(TOK if last else 384),
        scratch_shapes=[pltpu.VMEM((128, WID), F32)] if last else [],
        compiler_params=pltpu.CompilerParams(vmem_limit_bytes=LIMIT),
        cost_estimate=pl.CostEstimate(
            flops=2 * 128 * len(blocks) * WID * FFL, bytes_accessed=2 * (TOK + WID) * FFL, transcendentals=0
        ),
        name="far_input_grads" if last else "near_input_grads",
    )(*((order,) if last else ()), w_in, *blocks, *((near,) if last else ()))


def near_weight_kernel(outer, rows_ref, b0_ref, b1_ref, b3_ref, out_ref):
    rows = jnp.concatenate([rows_ref[:256], rows_ref[384:]], axis=0)
    block = jnp.concatenate([b0_ref[...], b1_ref[...], b3_ref[...]], axis=0)
    pair = (block, rows) if outer else (rows, block)
    out_ref[...] = lax.dot_general(*pair, (((0,), (0,)), ((), ())), preferred_element_type=F32).astype(BF16)


def far_weight_kernel(outer, rows_ref, left_ref, right_ref, near_ref, out_ref):
    rows, block = rows_ref[256:384], chosen(left_ref, right_ref)
    pair = (block, rows) if outer else (rows, block)
    term = lax.dot_general(*pair, (((0,), (0,)), ((), ())), preferred_element_type=F32)
    out_ref[...] = (near_ref[...].astype(F32) + term).astype(BF16)


def weight_grads(outer, rows, blocks, near=None):
    last = near is not None
    spec = (
        pl.BlockSpec((TILE, WID), lambda i: (i, 0)) if outer else pl.BlockSpec((WID, TILE), lambda i: (0, i))
    )
    return pl.pallas_call(
        functools.partial(far_weight_kernel if last else near_weight_kernel, outer),
        grid=(TILES,),
        out_shape=jax.ShapeDtypeStruct((FFL, WID) if outer else (WID, FFL), BF16),
        in_specs=[pl.BlockSpec((TOK, WID), lambda i: (0, 0))]
        + block_specs(last, blocks)
        + [spec] * last,
        out_specs=spec,
        compiler_params=pltpu.CompilerParams(vmem_limit_bytes=LIMIT),
        cost_estimate=pl.CostEstimate(flops=TOK * WID, bytes_accessed=TOK * WID, transcendentals=0),
        name=("far_" if last else "near_") + ("grad_w_out" if outer else "grad_w_in"),
    )(rows, *blocks, *((near,) if last else ()))


class Stream:
    def __init__(self, hidden, tokens, weight):
        self.hidden, self.own, self.weight = hidden, tokens, weight

    def gather_z(self, env):
        steps = (2, 1, -1) if self.hidden else (1, -1)
        self.came = tuple(hop_z(self.own, step) for step in steps)

    def gather_z_far(self, env):
        self.came = hop_z(env.after(self.own), 2), *self.came

    def gather_core(self, env):
        own, far, left, right = env.after((self.own, *self.came))
        own = jnp.concatenate([own, right, far, left], axis=0)
        self.came = swap_core(own)
        self.own = stage(own) if self.hidden else own
        return (self.own,)

    def partials(self, env):
        tokens = jnp.concatenate([self.own, env.after(self.came)], axis=0)
        self.rows, *parts = partials(self.hidden, env.order, tokens, self.weight)
        self.far_left, self.far_right, self.p1, self.p3, self.p0 = parts
        return parts

    def send_far(self, env):
        left, right = env.after((self.far_left, self.far_right))
        self.came = hop(left, 1, True), hop(right, -1, True)

    def send_near(self, env):
        from_left, from_right = env.after(self.came)
        right = jnp.concatenate([add(self.p1[:, :HALF], from_left).astype(BF16), self.p1[:, HALF:]], axis=1)
        left = jnp.concatenate([self.p3[:, :HALF], add(self.p3[:, HALF:], from_right).astype(BF16)], axis=1)
        self.came = hop(right, 1, True), hop(left, -1, True)
        return right, left

    def send_second(self, env):
        from_left, from_right = env.after(self.came)
        q = add(self.p0, from_left, from_right).astype(BF16)
        blocks = [q[32 * i : 32 * (i + 1)] for i in range(4)]
        self.own = blocks[0]
        self.came = tuple(hop(blocks[i], step, False) for i, step in ((3, -1), (1, 1), (2, 2)))
        return (q,)

    def sum_second(self, env):
        self.own = add(self.own, *env.after(self.came))
        return (self.own,)

    def send_own(self):
        self.came = tuple(hop(self.own, step, False) for step in (-1, 1, 2))

    def gather_near(self, env):
        right, left, far = env.after(self.came)
        self.quarter = jnp.concatenate([self.own, right, far, left], axis=0)
        self.came = hop(self.quarter, 1, True), hop(self.quarter, -1, True)
        return (self.quarter,)

    def gather_far(self, env):
        self.left, self.right = env.after(self.came)
        halves = self.left[:, :HALF], self.right[:, HALF:]
        self.came = hop(halves[0], 1, True), hop(halves[1], -1, True)
        return halves

    def near(self):
        return self.quarter, self.right, self.left

    def far(self, env):
        return env.after(self.came)


class Env:
    def __init__(self, **given):
        self.__dict__.update(given)
        self.last = ()

    def after(self, values):
        return lax.optimization_barrier((values, self.last))[0] if self.last else values

    def activate(self, env):
        activated, derivative = gelu_parts(self.h.own)
        self.h.own, self.g.own = activated.astype(BF16), (self.g.own * derivative).astype(BF16)
        self.g.send_own()
        self.h.send_own()
        return self.g.own, self.h.own

    def near_input_grads(self, env):
        self.near = input_grads(self.w_in, env.after(self.g.near()))
        return (self.near,)

    def near_grad_w_in(self, env):
        self.near_w_in = weight_grads(False, env.after(self.h.rows), self.g.near())
        return (self.near_w_in,)

    def near_grad_w_out(self, env):
        self.near_w_out = weight_grads(True, env.after(self.g.rows), self.h.near())
        return (self.near_w_out,)

    def far_input_grads(self, env):
        self.g_far = self.g.far(env)
        sums = input_grads(self.w_in, self.g_far, self.near, self.order)
        self.sums = sums.reshape(2, N_Z, 64, WID)
        self.swapped = swap_core(self.sums[1])
        return (self.sums,)

    def grad_w_in(self, env):
        self.w_in_result = weight_grads(False, env.after(self.h.rows), self.g_far, self.near_w_in)
        return (self.w_in_result,)

    def grad_w_out(self, env):
        self.w_out_result = weight_grads(True, self.g.rows, self.h.far(env), self.near_w_out)
        return (self.w_out_result,)

    def sum_cores(self, env):
        total = add(self.sums[0], env.after(self.swapped)).astype(BF16)
        self.kept = total[0]
        self.crossed = tuple(hop_z(total[step % N_Z], step) for step in (2, 1, -1))
        return (total,)

    def sum_z(self, env):
        self.inputs_result = add(self.kept, *env.after(self.crossed)).astype(BF16)
        return (self.inputs_result,)


def shards(inputs, cotangent, w_in, w_out):
    row, col = lax.axis_index("row"), lax.axis_index("col")
    x, y, z, core = row // N_Y, row % N_Y, col // N_C, col % N_C
    o = jnp.arange(16, dtype=jnp.int32)
    ox = jnp.where(core == 0, o // 4, o % 4)
    oy = jnp.where(core == 0, o % 4, o // 4)
    block = ((x + ox) % N_X) * N_Y + (y + oy) % N_Y
    other = (block // 2 + core) % N_C
    order = (other * N_Z + (block // 4 - z) % N_Z) * 2 + block % 2

    env = Env(order=order, w_in=w_in, h=Stream(True, inputs, w_in), g=Stream(False, cotangent, w_out))
    for where, step in STEPS:
        env.last = getattr(getattr(env, where) if where else env, step)(env) or env.last
    return env.inputs_result, env.w_in_result, env.w_out_result


def solution(mesh):
    in_specs = (P("col", "row"), P("col", "row"), P("row", "col"), P("col", "row"))
    out_specs = (P("col", "row"), P("row", "col"), P("col", "row"))
    return jax.shard_map(shards, mesh=mesh, in_specs=in_specs, out_specs=out_specs, check_vma=False)
```

```python
import functools
import math

import jax
import jax.numpy as jnp
from jax import lax
from jax.experimental import pallas as pl
from jax.experimental.pallas import tpu as pltpu
from jax.sharding import PartitionSpec as P

N_X, N_Y, N_Z, N_C = 4, 4, 4, 2
TOK, WID, FFL = 512, 640, 5120
HALF = FFL // 2
TILE = 2560
TILES = FFL // TILE
AXES = ("row", "col")
F32, BF16 = jnp.float32, jnp.bfloat16
LIMIT = 24 * 2**20
STEPS = (
    ("h", "gather_z"),
    ("g", "gather_z"),
    ("h", "gather_core"),
    ("g", "gather_z_far"),
    ("h", "partials"),
    ("g", "gather_core"),
    ("h", "send_far"),
    ("g", "partials"),
    ("g", "send_far"),
    ("h", "send_near"),
    ("g", "send_near"),
    ("h", "send_second"),
    ("g", "send_second"),
    ("h", "sum_second"),
    ("g", "sum_second"),
    ("", "activate"),
    ("g", "gather_near"),
    ("h", "gather_near"),
    ("g", "gather_far"),
    ("", "near_input_grads"),
    ("", "near_grad_w_in"),
    ("h", "gather_far"),
    ("", "near_grad_w_out"),
    ("", "far_input_grads"),
    ("", "grad_w_in_left"),
    ("", "take_far"),
    ("", "sum_cores"),
    ("", "grad_w_out"),
    ("", "grad_w_in_right"),
    ("", "sum_z"),
)


def neighbours(move):
    pairs = []
    for x in range(N_X):
        for y in range(N_Y):
            for z in range(N_Z):
                for c in range(N_C):
                    nx, ny, nz, nc = move(x, y, z, c)
                    here = ((x * N_Y + y) * N_Z + z) * N_C + c
                    there = (((nx % N_X) * N_Y + ny % N_Y) * N_Z + nz % N_Z) * N_C + nc % N_C
                    pairs.append((here, there))
    return pairs


def hop(value, step, first):
    def move(x, y, z, c):
        return (x + step, y, z, c) if (c == 0) == first else (x, y + step, z, c)

    return lax.ppermute(value, AXES, neighbours(move))


def hop_z(value, step):
    return lax.ppermute(value, AXES, neighbours(lambda x, y, z, c: (x, y, z + step, c)))


def swap_core(value):
    return lax.ppermute(value, AXES, neighbours(lambda x, y, z, c: (x, y, z, c + 1)))


def add(*terms):
    total = terms[0].astype(F32)
    for term in terms[1:]:
        total = total + term.astype(F32)
    return total


def gelu_parts(hidden):
    normal_cdf = 0.5 * (1.0 + jax.scipy.special.erf(hidden / math.sqrt(2.0)))
    density = jnp.exp(-0.5 * hidden * hidden) / math.sqrt(2.0 * math.pi)
    return (hidden * normal_cdf, normal_cdf + hidden * density)


def store_partials(term, far_left_ref, far_right_ref, p1_ref, p3_ref, p0_ref):
    tile = pl.program_id(0)
    p0_ref[...] = term[0:128]
    p1_ref[...] = term[128:256]
    p3_ref[...] = term[384:512]

    @pl.when(tile < TILES // 2)
    def _():
        far_left_ref[...] = term[256:384]

    @pl.when(tile >= TILES // 2)
    def _():
        far_right_ref[...] = term[256:384]


def partial_kernel(hidden, order_ref, all_ref, w_ref, rows_ref, *outs):
    @pl.when(pl.program_id(0) == 0)
    def _():
        for block in range(16):
            start = pl.multiple_of(order_ref[block] * 32, 32)
            rows_ref[block * 32 : (block + 1) * 32, :] = all_ref[pl.ds(start, 32), :]

    sides = (((1,), (0 if hidden else 1,)), ((), ()))
    term = lax.dot_general(rows_ref[...], w_ref[...], sides, preferred_element_type=F32)
    store_partials(term.astype(BF16), *outs)


def partials(hidden, order, tokens, weight):
    whole = pl.BlockSpec((TOK, WID), lambda i: (0, 0))
    rows = jax.ShapeDtypeStruct((TOK, WID), BF16)
    half = jax.ShapeDtypeStruct((128, HALF), BF16)
    block = jax.ShapeDtypeStruct((128, FFL), BF16)
    spec = pl.BlockSpec((128, TILE), lambda i: (0, i))
    left = pl.BlockSpec((128, TILE), lambda i: (0, jnp.minimum(i, TILES // 2 - 1)))
    right = pl.BlockSpec((128, TILE), lambda i: (0, jnp.maximum(i - TILES // 2, 0)))
    return pl.pallas_call(
        functools.partial(partial_kernel, hidden),
        grid=(TILES,),
        out_shape=(rows, half, half, block, block, block),
        in_specs=[
            pl.BlockSpec(memory_space=pltpu.SMEM),
            whole,
            pl.BlockSpec((WID, TILE), lambda i: (0, i))
            if hidden
            else pl.BlockSpec((TILE, WID), lambda i: (i, 0)),
        ],
        out_specs=(whole, left, right, spec, spec, spec),
        compiler_params=pltpu.CompilerParams(vmem_limit_bytes=LIMIT),
        cost_estimate=pl.CostEstimate(
            flops=2 * TOK * WID * FFL, bytes_accessed=2 * (TOK + WID) * FFL, transcendentals=0
        ),
        name="hidden_partials" if hidden else "grad_partials",
    )(order, tokens, weight)


def stage_kernel(source_ref, target_ref):
    target_ref[...] = source_ref[...]


def stage(rows):
    return pl.pallas_call(
        stage_kernel,
        out_shape=jax.ShapeDtypeStruct(rows.shape, rows.dtype),
        compiler_params=pltpu.CompilerParams(vmem_limit_bytes=LIMIT),
        cost_estimate=pl.CostEstimate(
            flops=4 * TOK * WID * FFL, bytes_accessed=4 * WID * FFL, transcendentals=0
        ),
        name="stage",
    )(rows)


def near_input_grads_kernel(wi_ref, b0_ref, b1_ref, b3_ref, out_ref):
    @pl.when(pl.program_id(0) == 0)
    def _():
        out_ref[...] = jnp.zeros_like(out_ref)

    grad = jnp.concatenate([b0_ref[...], b1_ref[...], b3_ref[...]], axis=0)
    out_ref[...] += lax.dot_general(grad, wi_ref[...], (((1,), (1,)), ((), ())), preferred_element_type=F32)


def chosen(left_ref, right_ref):
    return jnp.where(pl.program_id(0) < TILES // 2, left_ref[...], right_ref[...])


def far_input_grads_kernel(order_ref, wi_ref, left_ref, right_ref, near_ref, out_ref, total):
    @pl.when(pl.program_id(0) == 0)
    def _():
        total[...] = jnp.zeros_like(total)

    total[...] += lax.dot_general(
        chosen(left_ref, right_ref), wi_ref[...], (((1,), (1,)), ((), ())), preferred_element_type=F32
    )

    @pl.when(pl.program_id(0) == pl.num_programs(0) - 1)
    def _():
        for block in range(16):
            rows = pl.ds(pl.multiple_of(order_ref[block] * 32, 32), 32)
            low = (block % 4) * 32
            if block // 4 == 2:
                term = total[low : low + 32, :]
            else:
                low += (0, 128, 0, 256)[block // 4]
                term = near_ref[low : low + 32, :]
            out_ref[rows, :] = term.astype(BF16)


def block_specs(last, blocks):
    if not last:
        return [pl.BlockSpec((128, TILE), lambda i: (0, i)) for _ in blocks]
    return [
        pl.BlockSpec((128, TILE), lambda i: (0, jnp.minimum(i, TILES // 2 - 1))),
        pl.BlockSpec((128, TILE), lambda i: (0, jnp.maximum(i - TILES // 2, 0))),
    ]


def input_grads(w_in, blocks, near=None, order=None):
    last = near is not None
    whole = lambda rows: pl.BlockSpec((rows, WID), lambda i: (0, 0))
    return pl.pallas_call(
        far_input_grads_kernel if last else near_input_grads_kernel,
        grid=(TILES,),
        out_shape=jax.ShapeDtypeStruct((TOK, WID), BF16) if last else jax.ShapeDtypeStruct((384, WID), F32),
        in_specs=([pl.BlockSpec(memory_space=pltpu.SMEM)] if last else [])
        + [pl.BlockSpec((WID, TILE), lambda i: (0, i))]
        + block_specs(last, blocks)
        + ([whole(384)] if last else []),
        out_specs=whole(TOK if last else 384),
        scratch_shapes=[pltpu.VMEM((128, WID), F32)] if last else [],
        compiler_params=pltpu.CompilerParams(vmem_limit_bytes=LIMIT),
        cost_estimate=pl.CostEstimate(
            flops=2 * 128 * len(blocks) * WID * FFL, bytes_accessed=2 * (TOK + WID) * FFL, transcendentals=0
        ),
        name="far_input_grads" if last else "near_input_grads",
    )(*((order,) if last else ()), w_in, *blocks, *((near,) if last else ()))


def near_weight_kernel(outer, rows_ref, b0_ref, b1_ref, b3_ref, out_ref):
    rows = jnp.concatenate([rows_ref[:256], rows_ref[384:]], axis=0)
    block = jnp.concatenate([b0_ref[...], b1_ref[...], b3_ref[...]], axis=0)
    pair = (block, rows) if outer else (rows, block)
    out_ref[...] = lax.dot_general(*pair, (((0,), (0,)), ((), ())), preferred_element_type=F32).astype(BF16)


def far_weight_kernel(outer, rows_ref, left_ref, right_ref, near_ref, out_ref):
    rows, block = rows_ref[256:384], chosen(left_ref, right_ref)
    pair = (block, rows) if outer else (rows, block)
    term = lax.dot_general(*pair, (((0,), (0,)), ((), ())), preferred_element_type=F32)
    out_ref[...] = (near_ref[...].astype(F32) + term).astype(BF16)


def weight_grads(outer, rows, blocks, near=None):
    last = near is not None
    spec = (
        pl.BlockSpec((TILE, WID), lambda i: (i, 0)) if outer else pl.BlockSpec((WID, TILE), lambda i: (0, i))
    )
    return pl.pallas_call(
        functools.partial(far_weight_kernel if last else near_weight_kernel, outer),
        grid=(TILES,),
        out_shape=jax.ShapeDtypeStruct((FFL, WID) if outer else (WID, FFL), BF16),
        in_specs=[pl.BlockSpec((TOK, WID), lambda i: (0, 0))]
        + block_specs(last, blocks)
        + [spec] * last,
        out_specs=spec,
        compiler_params=pltpu.CompilerParams(vmem_limit_bytes=LIMIT),
        cost_estimate=pl.CostEstimate(flops=TOK * WID, bytes_accessed=TOK * WID, transcendentals=0),
        name=("far_" if last else "near_") + ("grad_w_out" if outer else "grad_w_in"),
    )(rows, *blocks, *((near,) if last else ()))


def far_half_kernel(rows_ref, b2_ref, near_ref, *rest):
    term = lax.dot_general(
        rows_ref[256:384], b2_ref[...], (((0,), (0,)), ((), ())), preferred_element_type=F32
    )
    rest[-1][...] = (near_ref[...].astype(F32) + term).astype(BF16)


def far_grad_w_in(rows, half, near, base, before=()):
    spec = pl.BlockSpec((WID, TILE), lambda i: (0, base + i))
    return pl.pallas_call(
        far_half_kernel,
        grid=(TILES // 2,),
        out_shape=jax.ShapeDtypeStruct((WID, FFL), BF16),
        in_specs=[
            pl.BlockSpec((TOK, WID), lambda i: (0, 0)),
            pl.BlockSpec((128, TILE), lambda i: (0, i)),
            spec,
        ]
        + [pl.BlockSpec(memory_space=pl.ANY)] * len(before),
        out_specs=spec,
        input_output_aliases={3: 0} if before else {},
        compiler_params=pltpu.CompilerParams(vmem_limit_bytes=LIMIT),
        cost_estimate=pl.CostEstimate(flops=TOK * WID, bytes_accessed=TOK * WID, transcendentals=0),
        name="far_grad_w_in",
    )(rows, half, near, *before)


class Stream:
    def __init__(self, hidden, tokens, weight):
        self.hidden, self.own, self.weight = hidden, tokens, weight

    def gather_z(self, env):
        steps = (2, 1, -1) if self.hidden else (1, -1)
        self.came = tuple(hop_z(self.own, step) for step in steps)

    def gather_z_far(self, env):
        self.came = hop_z(env.after(self.own), 2), *self.came

    def gather_core(self, env):
        own, far, left, right = env.after((self.own, *self.came))
        own = jnp.concatenate([own, right, far, left], axis=0)
        self.came = swap_core(own)
        self.own = stage(own) if self.hidden else own
        return (self.own,)

    def partials(self, env):
        tokens = jnp.concatenate([self.own, env.after(self.came)], axis=0)
        self.rows, *parts = partials(self.hidden, env.order, tokens, self.weight)
        self.far_left, self.far_right, self.p1, self.p3, self.p0 = parts
        return parts

    def send_far(self, env):
        left, right = env.after((self.far_left, self.far_right))
        self.came = hop(left, 1, True), hop(right, -1, True)

    def send_near(self, env):
        from_left, from_right = env.after(self.came)
        right = jnp.concatenate([add(self.p1[:, :HALF], from_left).astype(BF16), self.p1[:, HALF:]], axis=1)
        left = jnp.concatenate([self.p3[:, :HALF], add(self.p3[:, HALF:], from_right).astype(BF16)], axis=1)
        self.came = hop(right, 1, True), hop(left, -1, True)
        return right, left

    def send_second(self, env):
        from_left, from_right = env.after(self.came)
        q = add(self.p0, from_left, from_right).astype(BF16)
        blocks = [q[32 * i : 32 * (i + 1)] for i in range(4)]
        self.own = blocks[0]
        self.came = tuple(hop(blocks[i], step, False) for i, step in ((3, -1), (1, 1), (2, 2)))
        return (q,)

    def sum_second(self, env):
        self.own = add(self.own, *env.after(self.came))
        return (self.own,)

    def send_own(self):
        self.came = tuple(hop(self.own, step, False) for step in (-1, 1, 2))

    def gather_near(self, env):
        right, left, far = env.after(self.came)
        self.quarter = jnp.concatenate([self.own, right, far, left], axis=0)
        self.came = hop(self.quarter, 1, True), hop(self.quarter, -1, True)
        return (self.quarter,)

    def gather_far(self, env):
        self.left, self.right = env.after(self.came)
        halves = self.left[:, :HALF], self.right[:, HALF:]
        self.came = hop(halves[0], 1, True), hop(halves[1], -1, True)
        return halves

    def near(self):
        return self.quarter, self.right, self.left

    def far(self, env):
        return env.after(self.came)


class Env:
    def __init__(self, **given):
        self.__dict__.update(given)
        self.last = ()

    def after(self, values):
        return lax.optimization_barrier((values, self.last))[0] if self.last else values

    def activate(self, env):
        activated, derivative = gelu_parts(self.h.own)
        self.h.own, self.g.own = activated.astype(BF16), (self.g.own * derivative).astype(BF16)
        self.g.send_own()
        self.h.send_own()
        return self.g.own, self.h.own

    def near_input_grads(self, env):
        self.near = input_grads(self.w_in, env.after(self.g.near()))
        return (self.near,)

    def near_grad_w_in(self, env):
        self.near_w_in = weight_grads(False, env.after(self.h.rows), self.g.near())
        return (self.near_w_in,)

    def near_grad_w_out(self, env):
        self.near_w_out = weight_grads(True, env.after(self.g.rows), self.h.near())
        return (self.near_w_out,)

    def far_input_grads(self, env):
        self.g_far = self.g.far(env)
        sums = input_grads(self.w_in, self.g_far, self.near, self.order)
        self.sums = sums.reshape(2, N_Z, 64, WID)
        self.swapped = swap_core(self.sums[1])
        return (self.sums,)

    def grad_w_in_left(self, env):
        rows = env.after(self.h.rows)
        self.w_in_left = far_grad_w_in(rows, self.g_far[0], self.near_w_in, 0)
        return (self.w_in_left,)

    def grad_w_in_right(self, env):
        rows = env.after(self.h.rows)
        self.w_in_result = far_grad_w_in(rows, self.g_far[1], self.near_w_in, TILES // 2, (self.w_in_left,))
        return (self.w_in_result,)

    def take_far(self, env):
        self.h_far = self.h.far(env)
        return self.h_far

    def grad_w_out(self, env):
        self.w_out_result = weight_grads(True, env.after(self.g.rows), self.h_far, self.near_w_out)
        return (self.w_out_result,)

    def sum_cores(self, env):
        total = add(self.sums[0], env.after(self.swapped)).astype(BF16)
        self.kept = total[0]
        self.crossed = tuple(hop_z(total[step % N_Z], step) for step in (2, 1, -1))
        return (total,)

    def sum_z(self, env):
        self.inputs_result = add(self.kept, *env.after(self.crossed)).astype(BF16)
        return (self.inputs_result,)


def shards(inputs, cotangent, w_in, w_out):
    row, col = lax.axis_index("row"), lax.axis_index("col")
    x, y, z, core = row // N_Y, row % N_Y, col // N_C, col % N_C
    o = jnp.arange(16, dtype=jnp.int32)
    ox = jnp.where(core == 0, o // 4, o % 4)
    oy = jnp.where(core == 0, o % 4, o // 4)
    block = ((x + ox) % N_X) * N_Y + (y + oy) % N_Y
    other = (block // 2 + core) % N_C
    order = (other * N_Z + (block // 4 - z) % N_Z) * 2 + block % 2

    env = Env(order=order, w_in=w_in, h=Stream(True, inputs, w_in), g=Stream(False, cotangent, w_out))
    for where, step in STEPS:
        env.last = getattr(getattr(env, where) if where else env, step)(env) or env.last
    return env.inputs_result, env.w_in_result, env.w_out_result


def solution(mesh):
    in_specs = (P("col", "row"), P("col", "row"), P("row", "col"), P("col", "row"))
    out_specs = (P("col", "row"), P("row", "col"), P("col", "row"))
    return jax.shard_map(shards, mesh=mesh, in_specs=in_specs, out_specs=out_specs, check_vma=False)
```

```python
import functools
import math

import jax
import jax.numpy as jnp
from jax import lax
from jax.experimental import pallas as pl
from jax.experimental.pallas import tpu as pltpu
from jax.sharding import PartitionSpec as P

N_X, N_Y, N_Z, N_C = 4, 4, 4, 2
TOK, WID, FFL = 512, 640, 5120
HALF = FFL // 2
TILE = 2560
TILES = FFL // TILE
AXES = ("row", "col")
F32, BF16 = jnp.float32, jnp.bfloat16
LIMIT = 24 * 2**20
STEPS = (
    ("h", "gather_z"),
    ("g", "gather_z"),
    ("h", "gather_core"),
    ("g", "gather_z_far"),
    ("h", "partials"),
    ("g", "gather_core"),
    ("h", "send_far"),
    ("g", "partials"),
    ("g", "send_far"),
    ("h", "send_near"),
    ("g", "send_near"),
    ("h", "send_second"),
    ("g", "send_second"),
    ("h", "sum_second"),
    ("g", "sum_second"),
    ("", "activate"),
    ("g", "gather_near"),
    ("h", "gather_near"),
    ("g", "gather_far"),
    ("", "near_input_grads"),
    ("", "near_grad_w_in"),
    ("h", "gather_far"),
    ("", "near_grad_w_out"),
    ("", "far_input_grads"),
    ("", "grad_w_in_left"),
    ("", "take_far"),
    ("", "sum_cores"),
    ("", "last_grads"),
    ("", "sum_z"),
)


def neighbours(move):
    pairs = []
    for x in range(N_X):
        for y in range(N_Y):
            for z in range(N_Z):
                for c in range(N_C):
                    nx, ny, nz, nc = move(x, y, z, c)
                    here = ((x * N_Y + y) * N_Z + z) * N_C + c
                    there = (((nx % N_X) * N_Y + ny % N_Y) * N_Z + nz % N_Z) * N_C + nc % N_C
                    pairs.append((here, there))
    return pairs


def hop(value, step, first):
    def move(x, y, z, c):
        return (x + step, y, z, c) if (c == 0) == first else (x, y + step, z, c)

    return lax.ppermute(value, AXES, neighbours(move))


def hop_z(value, step):
    return lax.ppermute(value, AXES, neighbours(lambda x, y, z, c: (x, y, z + step, c)))


def swap_core(value):
    return lax.ppermute(value, AXES, neighbours(lambda x, y, z, c: (x, y, z, c + 1)))


def add(*terms):
    total = terms[0].astype(F32)
    for term in terms[1:]:
        total = total + term.astype(F32)
    return total


def gelu_parts(hidden):
    normal_cdf = 0.5 * (1.0 + jax.scipy.special.erf(hidden / math.sqrt(2.0)))
    density = jnp.exp(-0.5 * hidden * hidden) / math.sqrt(2.0 * math.pi)
    return (hidden * normal_cdf, normal_cdf + hidden * density)


def store_partials(term, far_left_ref, far_right_ref, p1_ref, p3_ref, p0_ref):
    tile = pl.program_id(0)
    p0_ref[...] = term[0:128]
    p1_ref[...] = term[128:256]
    p3_ref[...] = term[384:512]

    @pl.when(tile < TILES // 2)
    def _():
        far_left_ref[...] = term[256:384]

    @pl.when(tile >= TILES // 2)
    def _():
        far_right_ref[...] = term[256:384]


def partial_kernel(hidden, order_ref, all_ref, w_ref, rows_ref, *outs):
    @pl.when(pl.program_id(0) == 0)
    def _():
        for block in range(16):
            start = pl.multiple_of(order_ref[block] * 32, 32)
            rows_ref[block * 32 : (block + 1) * 32, :] = all_ref[pl.ds(start, 32), :]

    sides = (((1,), (0 if hidden else 1,)), ((), ()))
    term = lax.dot_general(rows_ref[...], w_ref[...], sides, preferred_element_type=F32)
    store_partials(term.astype(BF16), *outs)


def partials(hidden, order, tokens, weight):
    whole = pl.BlockSpec((TOK, WID), lambda i: (0, 0))
    rows = jax.ShapeDtypeStruct((TOK, WID), BF16)
    half = jax.ShapeDtypeStruct((128, HALF), BF16)
    block = jax.ShapeDtypeStruct((128, FFL), BF16)
    spec = pl.BlockSpec((128, TILE), lambda i: (0, i))
    left = pl.BlockSpec((128, TILE), lambda i: (0, jnp.minimum(i, TILES // 2 - 1)))
    right = pl.BlockSpec((128, TILE), lambda i: (0, jnp.maximum(i - TILES // 2, 0)))
    return pl.pallas_call(
        functools.partial(partial_kernel, hidden),
        grid=(TILES,),
        out_shape=(rows, half, half, block, block, block),
        in_specs=[
            pl.BlockSpec(memory_space=pltpu.SMEM),
            whole,
            pl.BlockSpec((WID, TILE), lambda i: (0, i))
            if hidden
            else pl.BlockSpec((TILE, WID), lambda i: (i, 0)),
        ],
        out_specs=(whole, left, right, spec, spec, spec),
        compiler_params=pltpu.CompilerParams(vmem_limit_bytes=LIMIT),
        cost_estimate=pl.CostEstimate(
            flops=2 * TOK * WID * FFL, bytes_accessed=2 * (TOK + WID) * FFL, transcendentals=0
        ),
        name="hidden_partials" if hidden else "grad_partials",
    )(order, tokens, weight)


def stage_kernel(source_ref, target_ref):
    target_ref[...] = source_ref[...]


def stage(rows):
    return pl.pallas_call(
        stage_kernel,
        out_shape=jax.ShapeDtypeStruct(rows.shape, rows.dtype),
        compiler_params=pltpu.CompilerParams(vmem_limit_bytes=LIMIT),
        cost_estimate=pl.CostEstimate(
            flops=4 * TOK * WID * FFL, bytes_accessed=4 * WID * FFL, transcendentals=0
        ),
        name="stage",
    )(rows)


def near_input_grads_kernel(wi_ref, b0_ref, b1_ref, b3_ref, out_ref):
    @pl.when(pl.program_id(0) == 0)
    def _():
        out_ref[...] = jnp.zeros_like(out_ref)

    grad = jnp.concatenate([b0_ref[...], b1_ref[...], b3_ref[...]], axis=0)
    out_ref[...] += lax.dot_general(grad, wi_ref[...], (((1,), (1,)), ((), ())), preferred_element_type=F32)


def chosen(left_ref, right_ref):
    return jnp.where(pl.program_id(0) < TILES // 2, left_ref[...], right_ref[...])


def far_input_grads_kernel(order_ref, wi_ref, left_ref, right_ref, near_ref, out_ref, total):
    @pl.when(pl.program_id(0) == 0)
    def _():
        total[...] = jnp.zeros_like(total)

    total[...] += lax.dot_general(
        chosen(left_ref, right_ref), wi_ref[...], (((1,), (1,)), ((), ())), preferred_element_type=F32
    )

    @pl.when(pl.program_id(0) == pl.num_programs(0) - 1)
    def _():
        for block in range(16):
            rows = pl.ds(pl.multiple_of(order_ref[block] * 32, 32), 32)
            low = (block % 4) * 32
            if block // 4 == 2:
                term = total[low : low + 32, :]
            else:
                low += (0, 128, 0, 256)[block // 4]
                term = near_ref[low : low + 32, :]
            out_ref[rows, :] = term.astype(BF16)


def block_specs(last, blocks):
    if not last:
        return [pl.BlockSpec((128, TILE), lambda i: (0, i)) for _ in blocks]
    return [
        pl.BlockSpec((128, TILE), lambda i: (0, jnp.minimum(i, TILES // 2 - 1))),
        pl.BlockSpec((128, TILE), lambda i: (0, jnp.maximum(i - TILES // 2, 0))),
    ]


def input_grads(w_in, blocks, near=None, order=None):
    last = near is not None
    whole = lambda rows: pl.BlockSpec((rows, WID), lambda i: (0, 0))
    return pl.pallas_call(
        far_input_grads_kernel if last else near_input_grads_kernel,
        grid=(TILES,),
        out_shape=jax.ShapeDtypeStruct((TOK, WID), BF16) if last else jax.ShapeDtypeStruct((384, WID), F32),
        in_specs=([pl.BlockSpec(memory_space=pltpu.SMEM)] if last else [])
        + [pl.BlockSpec((WID, TILE), lambda i: (0, i))]
        + block_specs(last, blocks)
        + ([whole(384)] if last else []),
        out_specs=whole(TOK if last else 384),
        scratch_shapes=[pltpu.VMEM((128, WID), F32)] if last else [],
        compiler_params=pltpu.CompilerParams(vmem_limit_bytes=LIMIT),
        cost_estimate=pl.CostEstimate(
            flops=2 * 128 * len(blocks) * WID * FFL, bytes_accessed=2 * (TOK + WID) * FFL, transcendentals=0
        ),
        name="far_input_grads" if last else "near_input_grads",
    )(*((order,) if last else ()), w_in, *blocks, *((near,) if last else ()))


def near_weight_kernel(outer, rows_ref, b0_ref, b1_ref, b3_ref, out_ref):
    rows = jnp.concatenate([rows_ref[:256], rows_ref[384:]], axis=0)
    block = jnp.concatenate([b0_ref[...], b1_ref[...], b3_ref[...]], axis=0)
    pair = (block, rows) if outer else (rows, block)
    out_ref[...] = lax.dot_general(*pair, (((0,), (0,)), ((), ())), preferred_element_type=F32).astype(BF16)


def far_weight_kernel(outer, rows_ref, left_ref, right_ref, near_ref, out_ref):
    rows, block = rows_ref[256:384], chosen(left_ref, right_ref)
    pair = (block, rows) if outer else (rows, block)
    term = lax.dot_general(*pair, (((0,), (0,)), ((), ())), preferred_element_type=F32)
    out_ref[...] = (near_ref[...].astype(F32) + term).astype(BF16)


def weight_grads(outer, rows, blocks, near=None):
    last = near is not None
    spec = (
        pl.BlockSpec((TILE, WID), lambda i: (i, 0)) if outer else pl.BlockSpec((WID, TILE), lambda i: (0, i))
    )
    return pl.pallas_call(
        functools.partial(far_weight_kernel if last else near_weight_kernel, outer),
        grid=(TILES,),
        out_shape=jax.ShapeDtypeStruct((FFL, WID) if outer else (WID, FFL), BF16),
        in_specs=[pl.BlockSpec((TOK, WID), lambda i: (0, 0))]
        + block_specs(last, blocks)
        + [spec] * last,
        out_specs=spec,
        compiler_params=pltpu.CompilerParams(vmem_limit_bytes=LIMIT),
        cost_estimate=pl.CostEstimate(flops=TOK * WID, bytes_accessed=TOK * WID, transcendentals=0),
        name=("far_" if last else "near_") + ("grad_w_out" if outer else "grad_w_in"),
    )(rows, *blocks, *((near,) if last else ()))


def far_half_kernel(rows_ref, b2_ref, near_ref, *rest):
    term = lax.dot_general(
        rows_ref[256:384], b2_ref[...], (((0,), (0,)), ((), ())), preferred_element_type=F32
    )
    rest[-1][...] = (near_ref[...].astype(F32) + term).astype(BF16)


def far_grad_w_in(rows, half, near, base, before=()):
    spec = pl.BlockSpec((WID, TILE), lambda i: (0, base + i))
    return pl.pallas_call(
        far_half_kernel,
        grid=(TILES // 2,),
        out_shape=jax.ShapeDtypeStruct((WID, FFL), BF16),
        in_specs=[
            pl.BlockSpec((TOK, WID), lambda i: (0, 0)),
            pl.BlockSpec((128, TILE), lambda i: (0, i)),
            spec,
        ]
        + [pl.BlockSpec(memory_space=pl.ANY)] * len(before),
        out_specs=spec,
        input_output_aliases={3: 0} if before else {},
        compiler_params=pltpu.CompilerParams(vmem_limit_bytes=LIMIT),
        cost_estimate=pl.CostEstimate(flops=TOK * WID, bytes_accessed=TOK * WID, transcendentals=0),
        name="far_grad_w_in",
    )(rows, half, near, *before)


STEP = 1280


def last_grads_kernel(c_ref, left_ref, right_ref, near_out_ref, x_ref, half_ref, near_in_ref, _, out_ref, in_ref):
    side = jnp.where(pl.program_id(0) < HALF // STEP, left_ref[...], right_ref[...])
    for rows, block, near_ref, target_ref in (
        (side, c_ref[256:384], near_out_ref, out_ref),
        (x_ref[256:384], half_ref[...], near_in_ref, in_ref),
    ):
        term = lax.dot_general(rows, block, (((0,), (0,)), ((), ())), preferred_element_type=F32)
        target_ref[...] = (near_ref[...].astype(F32) + term).astype(BF16)


def last_grads(c_all, far, near_out, x_all, half, near_in, before):
    steps, cut = FFL // STEP, HALF // STEP
    whole = pl.BlockSpec((TOK, WID), lambda i: (0, 0))
    out_spec = pl.BlockSpec((STEP, WID), lambda i: (i, 0))
    in_spec = pl.BlockSpec((WID, STEP // 2), lambda i: (0, steps + i))
    return pl.pallas_call(
        last_grads_kernel,
        grid=(steps,),
        out_shape=(jax.ShapeDtypeStruct((FFL, WID), BF16), jax.ShapeDtypeStruct((WID, FFL), BF16)),
        in_specs=[
            whole,
            pl.BlockSpec((128, STEP), lambda i: (0, jnp.minimum(i, cut - 1))),
            pl.BlockSpec((128, STEP), lambda i: (0, jnp.maximum(i - cut, 0))),
            out_spec,
            whole,
            pl.BlockSpec((128, STEP // 2), lambda i: (0, i)),
            in_spec,
            pl.BlockSpec(memory_space=pl.ANY),
        ],
        out_specs=(out_spec, in_spec),
        input_output_aliases={7: 1},
        compiler_params=pltpu.CompilerParams(vmem_limit_bytes=LIMIT),
        cost_estimate=pl.CostEstimate(flops=TOK * WID, bytes_accessed=TOK * WID, transcendentals=0),
        name="last_grads",
    )(c_all, *far, near_out, x_all, half, near_in, before)


class Stream:
    def __init__(self, hidden, tokens, weight):
        self.hidden, self.own, self.weight = hidden, tokens, weight

    def gather_z(self, env):
        steps = (2, 1, -1) if self.hidden else (1, -1)
        self.came = tuple(hop_z(self.own, step) for step in steps)

    def gather_z_far(self, env):
        self.came = hop_z(env.after(self.own), 2), *self.came

    def gather_core(self, env):
        own, far, left, right = env.after((self.own, *self.came))
        own = jnp.concatenate([own, right, far, left], axis=0)
        self.came = swap_core(own)
        self.own = stage(own) if self.hidden else own
        return (self.own,)

    def partials(self, env):
        tokens = jnp.concatenate([self.own, env.after(self.came)], axis=0)
        self.rows, *parts = partials(self.hidden, env.order, tokens, self.weight)
        self.far_left, self.far_right, self.p1, self.p3, self.p0 = parts
        return parts

    def send_far(self, env):
        left, right = env.after((self.far_left, self.far_right))
        self.came = hop(left, 1, True), hop(right, -1, True)

    def send_near(self, env):
        from_left, from_right = env.after(self.came)
        right = jnp.concatenate([add(self.p1[:, :HALF], from_left).astype(BF16), self.p1[:, HALF:]], axis=1)
        left = jnp.concatenate([self.p3[:, :HALF], add(self.p3[:, HALF:], from_right).astype(BF16)], axis=1)
        self.came = hop(right, 1, True), hop(left, -1, True)
        return right, left

    def send_second(self, env):
        from_left, from_right = env.after(self.came)
        q = add(self.p0, from_left, from_right).astype(BF16)
        blocks = [q[32 * i : 32 * (i + 1)] for i in range(4)]
        self.own = blocks[0]
        self.came = tuple(hop(blocks[i], step, False) for i, step in ((3, -1), (1, 1), (2, 2)))
        return (q,)

    def sum_second(self, env):
        self.own = add(self.own, *env.after(self.came))
        return (self.own,)

    def send_own(self):
        self.came = tuple(hop(self.own, step, False) for step in (-1, 1, 2))

    def gather_near(self, env):
        right, left, far = env.after(self.came)
        self.quarter = jnp.concatenate([self.own, right, far, left], axis=0)
        self.came = hop(self.quarter, 1, True), hop(self.quarter, -1, True)
        return (self.quarter,)

    def gather_far(self, env):
        self.left, self.right = env.after(self.came)
        halves = self.left[:, :HALF], self.right[:, HALF:]
        self.came = hop(halves[0], 1, True), hop(halves[1], -1, True)
        return halves

    def near(self):
        return self.quarter, self.right, self.left

    def far(self, env):
        return env.after(self.came)


class Env:
    def __init__(self, **given):
        self.__dict__.update(given)
        self.last = ()

    def after(self, values):
        return lax.optimization_barrier((values, self.last))[0] if self.last else values

    def activate(self, env):
        activated, derivative = gelu_parts(self.h.own)
        self.h.own, self.g.own = activated.astype(BF16), (self.g.own * derivative).astype(BF16)
        self.g.send_own()
        self.h.send_own()
        return self.g.own, self.h.own

    def near_input_grads(self, env):
        self.near = input_grads(self.w_in, env.after(self.g.near()))
        return (self.near,)

    def near_grad_w_in(self, env):
        self.near_w_in = weight_grads(False, env.after(self.h.rows), self.g.near())
        return (self.near_w_in,)

    def near_grad_w_out(self, env):
        self.near_w_out = weight_grads(True, env.after(self.g.rows), self.h.near())
        return (self.near_w_out,)

    def far_input_grads(self, env):
        self.g_far = self.g.far(env)
        sums = input_grads(self.w_in, self.g_far, self.near, self.order)
        self.sums = sums.reshape(2, N_Z, 64, WID)
        self.swapped = swap_core(self.sums[1])
        return (self.sums,)

    def grad_w_in_left(self, env):
        rows = env.after(self.h.rows)
        self.w_in_left = far_grad_w_in(rows, self.g_far[0], self.near_w_in, 0)
        return (self.w_in_left,)

    def take_far(self, env):
        self.h_far = self.h.far(env)
        return self.h_far

    def last_grads(self, env):
        self.w_out_result, self.w_in_result = last_grads(
            env.after(self.g.rows),
            self.h_far,
            self.near_w_out,
            self.h.rows,
            self.g_far[1],
            self.near_w_in,
            self.w_in_left,
        )
        return self.w_out_result, self.w_in_result

    def sum_cores(self, env):
        total = add(self.sums[0], env.after(self.swapped)).astype(BF16)
        self.kept = total[0]
        self.crossed = tuple(hop_z(total[step % N_Z], step) for step in (2, 1, -1))
        return (total,)

    def sum_z(self, env):
        self.inputs_result = add(self.kept, *env.after(self.crossed)).astype(BF16)
        return (self.inputs_result,)


def shards(inputs, cotangent, w_in, w_out):
    row, col = lax.axis_index("row"), lax.axis_index("col")
    x, y, z, core = row // N_Y, row % N_Y, col // N_C, col % N_C
    o = jnp.arange(16, dtype=jnp.int32)
    ox = jnp.where(core == 0, o // 4, o % 4)
    oy = jnp.where(core == 0, o % 4, o // 4)
    block = ((x + ox) % N_X) * N_Y + (y + oy) % N_Y
    other = (block // 2 + core) % N_C
    order = (other * N_Z + (block // 4 - z) % N_Z) * 2 + block % 2

    env = Env(order=order, w_in=w_in, h=Stream(True, inputs, w_in), g=Stream(False, cotangent, w_out))
    for where, step in STEPS:
        env.last = getattr(getattr(env, where) if where else env, step)(env) or env.last
    return env.inputs_result, env.w_in_result, env.w_out_result


def solution(mesh):
    in_specs = (P("col", "row"), P("col", "row"), P("row", "col"), P("col", "row"))
    out_specs = (P("col", "row"), P("row", "col"), P("col", "row"))
    return jax.shard_map(shards, mesh=mesh, in_specs=in_specs, out_specs=out_specs, check_vma=False)
```
